128 devices in a mesh: qx: 16 (over z, x), qy: 8 (over y, core).
Axes of the slice: x: 4, y: 4, z: 4, core: 2. Of those that a mesh axis runs over, the one named last changes fastest.
Arguments:
- dynamical: float32 [2, 64, 64, 9216], P(None, 'qx', 'qy'), may hold values from -0.15 to 1.5, as said below
Outputs:
- green_space: float32 [2, 64, 64, 9216], P(None, 'qx', 'qy')
The draws below stay inside these ranges and needn't reach their ends.
Inputs may be any that keep to these rules, and one draw needn't show every extreme that they name: `dynamical`: every q-point's matrix is Hermitian: the real part symmetric, the imaginary part antisymmetric with a zero diagonal; the real diagonal lies in 0.75 to 1.5.
All inputs are finite; a program needn't handle non-finite values.
Results may differ from the reference program's by a relative error of at most 0.00023.
Values sent between devices are 32-bit elements; how exact they have to be, the bound alone decides.
A program may use at most 64 MiB of HBM per device.

```python
import math
import jax
import jax.numpy as jnp
from jax import lax

M = 96
ITERS = 3
NX = 64
NY = 64


def draw_dynamical(key, part):
    key = jax.random.fold_in(key, 11)
    key_a, key_b, key_d = jax.random.split(key, 3)
    first = 0.035 * jax.random.truncated_normal(key_a, -4.0, 4.0, (NX, NY, M, M), jnp.float32)
    second = 0.035 * jax.random.truncated_normal(key_b, -4.0, 4.0, (NX, NY, M, M), jnp.float32)
    diag_vals = jax.random.uniform(key_d, (NX, NY, M), jnp.float32, 0.75, 1.5)
    identity = jnp.eye(M, dtype=jnp.float32)
    real_part = 0.5 * (first + jnp.swapaxes(first, 2, 3))
    real_part = real_part * (1.0 - identity) + identity * diag_vals[:, :, None, :]
    imag_part = 0.5 * (second - jnp.swapaxes(second, 2, 3))
    return jnp.stack([real_part.reshape(NX, NY, M * M), imag_part.reshape(NX, NY, M * M)])


def setup_inputs(seed: int = 0) -> dict:
    keys = jax.random.split(jax.random.key(seed), 2)
    dynamical = draw_dynamical(jax.random.fold_in(keys[1], 71), 0)
    return dict(dynamical=dynamical)


shift_eta = 0.25

def cmatmul(ar, ai, br, bi):
    hp = lax.Precision.HIGHEST
    real_part = jnp.matmul(ar, br, precision=hp) - jnp.matmul(ai, bi, precision=hp)
    imag_part = jnp.matmul(ar, bi, precision=hp) + jnp.matmul(ai, br, precision=hp)
    return (real_part, imag_part)

def newton_schulz(real_in, imag_in, size, steps):
    identity = jnp.eye(size, dtype=jnp.float32)
    diag_vals = jnp.diagonal(real_in, axis1=1, axis2=2)
    denom = diag_vals * diag_vals + shift_eta * shift_eta
    xr = identity[None] * (diag_vals / denom)[:, None, :]
    xi = identity[None] * (-shift_eta / denom)[:, None, :]
    ar = real_in
    ai = imag_in + shift_eta * identity[None]
    for step in range(steps):
        yr, yi = cmatmul(ar, ai, xr, xi)
        zr = 2.0 * identity[None] - yr
        zi = -yi
        xr, xi = cmatmul(xr, xi, zr, zi)
    return (xr, xi)

def tables(length):
    index = jnp.arange(length, dtype=jnp.int32)
    product = index[:, None] * index[None, :] % length
    angle = product.astype(jnp.float32) * (2.0 * math.pi / length)
    scale = 1.0 / math.sqrt(length)
    return (jnp.cos(angle) * scale, jnp.sin(angle) * scale)

def combine(cosine, sine, real, imag, form):
    hp = lax.Precision.HIGHEST
    out_r = jnp.einsum(form, cosine, real, precision=hp) - jnp.einsum(form, sine, imag, precision=hp)
    out_i = jnp.einsum(form, sine, real, precision=hp) + jnp.einsum(form, cosine, imag, precision=hp)
    return (out_r, out_i)

def reference(dynamical):

    def invert_row(row):
        real_in = row[0].reshape(NY, M, M)
        imag_in = row[1].reshape(NY, M, M)
        xr, xi = newton_schulz(real_in, imag_in, M, ITERS)
        return jnp.stack([xr.reshape(NY, M * M), xi.reshape(NY, M * M)])
    inverse = lax.map(invert_row, jnp.moveaxis(dynamical, 1, 0))
    inverse = jnp.moveaxis(inverse, 0, 1)
    cos_x, sin_x = tables(NX)
    ax_r, ax_i = combine(cos_x, sin_x, inverse[0], inverse[1], 'rq,qyk->ryk')
    cos_y, sin_y = tables(NY)
    gr, gi = combine(cos_y, sin_y, ax_r, ax_i, 'rq,xqk->xrk')
    return jnp.stack([gr, gi])
```

```python
import functools

import jax
import jax.numpy as jnp
import ml_dtypes
import numpy as np
from jax import lax
from jax.experimental import pallas as pl
from jax.experimental.pallas import tpu as pltpu
from jax.sharding import PartitionSpec as P

M = 96
ETA = 0.25
NDEV = 128
SIZE_X, SIZE_Y = 16, 8
LOCAL_X, LOCAL_Y = 4, 8
Q = LOCAL_X * LOCAL_Y
L = 128
ROWS = (8, 10)
PITCH = (16, 24)
USED = (16, 20)
MESH = pl.DeviceIdType.MESH
F32 = jnp.float32
BF16 = jnp.bfloat16


def split_table(table):
    high = table.astype(ml_dtypes.bfloat16)
    low = (table - high.astype(np.float64)).astype(ml_dtypes.bfloat16)
    return high, low


def embed_table(angle):
    cosine, sine = np.cos(angle), np.sin(angle)
    return np.block([[cosine, -sine], [sine, cosine]])


def tables():
    ax, ay = np.divmod(np.arange(NDEV), SIZE_Y)
    turns = (ax[:, None] * ax[None, :] % 16) / 16 + (ay[:, None] * ay[None, :] % 8) / 8
    first = np.concatenate(split_table(embed_table(2 * np.pi * turns)), axis=0)
    lane = np.arange(L)
    bx, by = lane % Q // LOCAL_Y, lane % LOCAL_Y
    turns = (ax[:, None] * bx[None, :] + ay[:, None] * by[None, :]) / 64
    twiddle = np.stack([np.cos(2 * np.pi * turns), np.sin(2 * np.pi * turns)]) / 64
    turns = (bx[:, None] * bx[None, :] % 4) / 4 + (by[:, None] * by[None, :] % 8) / 8
    same = (lane[:, None] // Q) == (lane[None, :] // Q)
    angle = 2 * np.pi * turns
    cosine, sine = np.cos(angle) * same, np.sin(angle) * same
    second = np.concatenate(split_table(np.block([[cosine, -sine], [sine, cosine]])), axis=0)
    return first, twiddle.astype(np.float32), second


def split(value):
    high = value.astype(BF16)
    low = (value - high.astype(F32)).astype(BF16)
    return high, low


def dot(a, b, contract=0):
    return lax.dot_general(a, b, (((1,), (contract,)), ((), ())), preferred_element_type=F32)


def embed(part):
    zeros = jnp.zeros((L - M, 2 * L), part.dtype)
    real, imag = part[:, :L], part[:, L:]
    return jnp.concatenate(
        [part, zeros, jnp.concatenate([-imag, real], axis=1), zeros], axis=0
    )


def product(left, right):
    n = left[0].shape[0]
    both = dot(jnp.concatenate(left, axis=0), embed(right[0]))
    return both[:n] + both[n:] + dot(left[0], embed(right[1]))


def invert(real, imag):
    row = lax.broadcasted_iota(jnp.int32, (M, L), 0)
    col = lax.broadcasted_iota(jnp.int32, (M, L), 1)
    eye = row == col
    off = (col < M) & (row != col)
    diag = jnp.where(eye, real, 0.0)

    def start(d):
        denom = d * d + ETA * ETA
        return d / denom, -ETA / denom

    cr, ci = start(jnp.sum(diag, axis=0, keepdims=True))
    rr, ri = start(jnp.sum(diag, axis=1, keepdims=True))
    er = jnp.where(off, imag * ci - real * cr, 0.0)
    ei = jnp.where(off, -(real * ci + imag * cr), 0.0)
    pr = jnp.where(eye, 1.0, er)
    x1 = jnp.concatenate([rr * pr - ri * ei, rr * ei + ri * pr], axis=1)
    e0 = split(jnp.concatenate([er, ei], axis=1))
    e1 = product(e0, e0)
    e1s = split(e1)
    x1s = split(x1)
    both = product(
        (jnp.concatenate([x1s[0], e1s[0]], axis=0), jnp.concatenate([x1s[1], e1s[1]], axis=0)), e1s
    )
    x2 = x1 + both[:M]
    return x2 + product(split(x2), split(both[M:]))


def kernel(
    d_ref, first_ref, twiddle_ref, second_ref, out_ref,
    mat, s0, s1, r0, r1, t0, t1, v0, v1, up_h, up_l, ssem, rsem, osem,
):
    qx = lax.axis_index("qx")
    qy = lax.axis_index("qy")
    me = qx * SIZE_Y + qy

    barrier = pltpu.get_barrier_semaphore()

    def greet(o, carry):
        other = lax.rem(me + o, NDEV)
        pl.semaphore_signal(
            barrier, inc=1, device_id=(other // SIZE_Y, lax.rem(other, SIZE_Y)), device_id_type=MESH
        )
        return carry

    lax.fori_loop(1, NDEV, greet, 0)

    def unflatten(n, carry):
        part, x = n // LOCAL_X, lax.rem(n, LOCAL_X)
        for i in range(M):
            first, last = i * M // L, min((i * M + L - 1) // L, 71)
            off = i * M % L
            tile = d_ref[part, x, :, first * L : (first + 1) * L]
            if off:
                lane = lax.broadcasted_iota(jnp.int32, (LOCAL_Y, L), 1)
                tile = pltpu.roll(tile, L - off, 1)
                if last > first:
                    after = pltpu.roll(d_ref[part, x, :, last * L : (last + 1) * L], L - off, 1)
                    tile = jnp.where(lane < L - off, tile, after)
            mat[part, pl.ds(x * LOCAL_Y * M + i, LOCAL_Y, stride=M), :] = tile
        return carry

    lax.fori_loop(0, 2 * LOCAL_X, unflatten, 0)

    def invert_one(n, carry):
        for k in range(2):
            rows = pl.ds(pl.multiple_of((2 * n + k) * M, M), M)
            result = invert(mat[0, rows, :], mat[1, rows, :])
            mat[0, rows, :] = result[:, :L]
            mat[1, rows, :] = result[:, L:]
        return carry

    lax.fori_loop(0, Q // 2, invert_one, 0)

    sends = (s0, s1)
    lands = (r0, r1)
    outs = (t0, t1)
    backs = (v0, v1)

    def exchange(src, dst, c, phase):
        used = pl.ds(0, USED[c])
        own = pltpu.make_async_copy(src.at[me, used], dst.at[me, used], rsem.at[phase, c])
        own.start()

        def send(o, carry):
            k = lax.rem(o, 4)
            core, a, b = lax.rem(o // 4, 2), lax.rem(o // 8, 4), o // 32
            z, x = qx // 4, lax.rem(qx, 4)
            y, h = qy // 2, lax.rem(qy, 2)
            tx = lax.rem(z + k, 4) * 4 + lax.rem(x + k + a, 4)
            ty = lax.rem(y + k + b, 4) * 2 + lax.rem(h + core, 2)
            target = tx * SIZE_Y + ty

            @pl.when(target != me)
            def _():
                pltpu.make_async_remote_copy(
                    src_ref=src.at[target, used],
                    dst_ref=dst.at[me, used],
                    send_sem=ssem.at[phase, c],
                    recv_sem=rsem.at[phase, c],
                    device_id=(tx, ty),
                    device_id_type=MESH,
                ).start()

            return carry

        lax.fori_loop(0, NDEV, send, 0)

    def arrived(dst, c, phase):
        whole = dst.at[:, pl.ds(0, USED[c])]
        pltpu.make_async_copy(whole, whole, rsem.at[phase, c]).wait()

    def sent(src, c, phase):
        whole = src.at[pl.ds(0, NDEV - 1), pl.ds(0, USED[c])]
        pltpu.make_async_copy(whole, whole, ssem.at[phase, c]).wait()

    def flat(ref, c):
        return ref.reshape(NDEV * PITCH[c], L)

    def pack(c, part, u, v, first_row):
        block = jnp.concatenate(
            [
                mat[part, pl.ds(16 * u + 4 * g + v, Q, stride=M), :]
                for g in range(4)
            ],
            axis=0,
        ).T
        for w in range(3):
            lo, hi = max(0, w * L - v * M), min(M, (w + 1) * L - v * M)
            if lo >= hi:
                continue
            row = 3 * u + w
            c = 0 if row < ROWS[0] else 1
            local = part * ROWS[c] + row - (0 if c == 0 else ROWS[0])
            target = v * M + lo - w * L
            flat(sends[c], c)[pl.ds(target * PITCH[c] + local, hi - lo, stride=PITCH[c]), :] = block[lo:hi]

    for u in range(6):
        for v in range(4):
            for part in range(2):
                pack(0, part, u, v, 0)
        if u == 2:
            pl.semaphore_wait(barrier, NDEV - 1)
            exchange(s0, r0, 0, 0)
    exchange(s1, r1, 1, 0)

    def stage_one(c, pair):
        src = flat(lands[c], c)
        cols = []
        for row in (2 * pair, 2 * pair + 1):
            cols.append(
                jnp.concatenate(
                    [src[pl.ds(part * ROWS[c] + row, NDEV, stride=PITCH[c]), :] for part in range(2)],
                    axis=0,
                )
            )
        high, low = split(jnp.concatenate(cols, axis=1))
        table = first_ref[...]
        both = dot(table, high)
        total = both[: 2 * L] + both[2 * L :] + dot(table[: 2 * L], low)
        tr, ti = twiddle_ref[0], twiddle_ref[1]
        for k in range(2):
            real, imag = total[:L, k * L : (k + 1) * L], total[L:, k * L : (k + 1) * L]
            yield jnp.concatenate([real * tr - imag * ti, real * ti + imag * tr], axis=1)

    def stage_two(c0, n):
        high, low = up_h[c0], up_l[c0]
        table = second_ref[...]
        both = dot(table, high, 1)
        return both[: 2 * L] + both[2 * L :] + dot(table[: 2 * L], low, 1)

    def transform(c):
        for pair in range(4):
            for k, rows in enumerate(stage_one(c, pair)):
                high, low = split(rows)
                row = 2 * pair + k
                for c0 in range(4):
                    up_h[c0, row * Q : (row + 1) * Q, :] = high[c0 * Q : (c0 + 1) * Q]
                    up_l[c0, row * Q : (row + 1) * Q, :] = low[c0 * Q : (c0 + 1) * Q]
        dst = flat(outs[c], c)
        for c0 in range(4):
            result = stage_two(c0, 0)
            for part in range(2):
                for g in range(4):
                    for jx in range(4):
                        r = part * L + g * Q + jx * 8
                        for quad in range(2):
                            dst[
                                pl.ds((4 * jx + c0) * 8 * PITCH[c] + part * 8 + g * 2 + quad, 8, stride=PITCH[c]), :
                            ] = result[r : r + 8, quad * L : (quad + 1) * L]
        if c == 0:
            return
        for k, rows in enumerate(stage_one(c, 4)):
            high, low = split(rows)
            for c0 in range(4):
                at = c0 * 2 * Q + k * Q
                up_h[0, at : at + Q, :] = high[c0 * Q : (c0 + 1) * Q]
                up_l[0, at : at + Q, :] = low[c0 * Q : (c0 + 1) * Q]
        result = stage_two(0, 0)
        lane = lax.broadcasted_iota(jnp.int32, (8, L), 1)
        for c0 in range(4):
            col = c0 // 2 * L
            for part in range(2):
                for gh in range(2):
                    for jx in range(4):
                        r = part * L + gh * 2 * Q + jx * 8
                        one = result[r : r + 8, col : col + L]
                        two = result[r + Q : r + Q + 8, col : col + L]
                        if c0 % 2 == 0:
                            row = jnp.where(lane < 64, one, pltpu.roll(two, 64, 1))
                        else:
                            row = jnp.where(lane < 64, pltpu.roll(one, 64, 1), two)
                        dst[
                            pl.ds((4 * jx + c0) * 8 * PITCH[c] + 16 + part * 2 + gh, 8, stride=PITCH[c]), :
                        ] = row

    def place(part, g, row, block):
        tile = 12 * (row // 3) + 3 * g + row % 3
        out_ref[part, :, :, tile * L : (tile + 1) * L] = block.reshape(LOCAL_X, LOCAL_Y, L)

    def finish(c):
        src = flat(backs[c], c)
        for part in range(2):
            for g in range(4):
                for quad in range(2):
                    block = src[pl.ds(part * 8 + g * 2 + quad, NDEV, stride=PITCH[c]), :].T
                    for k in range(4):
                        place(part, g, 8 * c + 4 * quad + k, block[k * Q : (k + 1) * Q])
            if c == 1:
                for gh in range(2):
                    block = src[pl.ds(16 + part * 2 + gh, NDEV, stride=PITCH[c]), :].T
                    for gl in range(2):
                        for k in range(2):
                            at = (2 * gl + k) * Q
                            place(part, 2 * gh + gl, 16 + k, block[at : at + Q])

    for c in range(2):
        arrived(lands[c], c, 0)
        transform(c)
        exchange(outs[c], backs[c], c, 1)
    for c in range(2):
        arrived(backs[c], c, 1)
        finish(c)
    for c in range(2):
        sent(sends[c], c, 0)
        sent(outs[c], c, 1)


def per_device(dynamical):
    vmem = pl.BlockSpec(memory_space=pltpu.VMEM)
    buffers = [pltpu.VMEM((NDEV, p, L), F32) for p in PITCH]
    return pl.pallas_call(
        kernel,
        out_shape=jax.ShapeDtypeStruct(dynamical.shape, F32),
        in_specs=[vmem] * 4,
        out_specs=vmem,
        scratch_shapes=[
            pltpu.VMEM((2, Q * M, L), F32),
            *buffers, *buffers, *buffers, *buffers,
            pltpu.VMEM((4, 2 * L, 2 * L), BF16),
            pltpu.VMEM((4, 2 * L, 2 * L), BF16),
            pltpu.SemaphoreType.DMA((2, 2)),
            pltpu.SemaphoreType.DMA((2, 2)),
            pltpu.SemaphoreType.REGULAR,
        ],
        compiler_params=pltpu.CompilerParams(
            collective_id=0, has_side_effects=True, vmem_limit_bytes=48 << 20
        ),
    )(dynamical, *tables())


def solution(mesh):
    return jax.shard_map(
        per_device,
        mesh=mesh,
        in_specs=(P(None, "qx", "qy", None),),
        out_specs=P(None, "qx", "qy", None),
        check_vma=False,
    )
```

```python
import functools

import jax
import jax.numpy as jnp
import ml_dtypes
import numpy as np
from jax import lax
from jax.experimental import pallas as pl
from jax.experimental.pallas import tpu as pltpu
from jax.sharding import PartitionSpec as P

M = 96
ETA = 0.25
NDEV = 128
SIZE_X, SIZE_Y = 16, 8
LOCAL_X, LOCAL_Y = 4, 8
Q = LOCAL_X * LOCAL_Y
L = 128
ROWS = (8, 10)
PITCH = (16, 24)
USED = (16, 20)
MESH = pl.DeviceIdType.MESH
F32 = jnp.float32
BF16 = jnp.bfloat16


def split_table(table):
    high = table.astype(ml_dtypes.bfloat16)
    low = (table - high.astype(np.float64)).astype(ml_dtypes.bfloat16)
    return high, low


def embed_table(angle):
    cosine, sine = np.cos(angle), np.sin(angle)
    return np.block([[cosine, -sine], [sine, cosine]])


def tables():
    ax, ay = np.divmod(np.arange(NDEV), SIZE_Y)
    turns = (ax[:, None] * ax[None, :] % 16) / 16 + (ay[:, None] * ay[None, :] % 8) / 8
    first = np.concatenate(split_table(embed_table(2 * np.pi * turns)), axis=0)
    lane = np.arange(L)
    bx, by = lane % Q // LOCAL_Y, lane % LOCAL_Y
    turns = (ax[:, None] * bx[None, :] + ay[:, None] * by[None, :]) / 64
    twiddle = np.stack([np.cos(2 * np.pi * turns), np.sin(2 * np.pi * turns)]) / 64
    turns = (bx[:, None] * bx[None, :] % 4) / 4 + (by[:, None] * by[None, :] % 8) / 8
    same = (lane[:, None] // Q) == (lane[None, :] // Q)
    angle = 2 * np.pi * turns
    cosine, sine = np.cos(angle) * same, np.sin(angle) * same
    second = np.concatenate(split_table(np.block([[cosine, -sine], [sine, cosine]])), axis=0)
    return first, twiddle.astype(np.float32), second


def split(value):
    high = value.astype(BF16)
    low = (value - high.astype(F32)).astype(BF16)
    return high, low


def dot(a, b, contract=0):
    return lax.dot_general(a, b, (((1,), (contract,)), ((), ())), preferred_element_type=F32)


def embed(part):
    zeros = jnp.zeros((L - M, 2 * L), part.dtype)
    real, imag = part[:, :L], part[:, L:]
    return jnp.concatenate(
        [part, zeros, jnp.concatenate([-imag, real], axis=1), zeros], axis=0
    )


def product(left, right):
    n = left[0].shape[0]
    both = dot(jnp.concatenate(left, axis=0), embed(right[0]))
    return both[:n] + both[n:] + dot(left[0], embed(right[1]))


def begin(real, imag):
    row = lax.broadcasted_iota(jnp.int32, (M, L), 0)
    col = lax.broadcasted_iota(jnp.int32, (M, L), 1)
    eye = row == col
    off = (col < M) & (row != col)
    diag = jnp.where(eye, real, 0.0)

    def start(d):
        denom = d * d + ETA * ETA
        return d / denom, -ETA / denom

    cr, ci = start(jnp.sum(diag, axis=0, keepdims=True))
    rr, ri = start(jnp.sum(diag, axis=1, keepdims=True))
    er = jnp.where(off, imag * ci - real * cr, 0.0)
    ei = jnp.where(off, -(real * ci + imag * cr), 0.0)
    pr = jnp.where(eye, 1.0, er)
    x1 = jnp.concatenate([rr * pr - ri * ei, rr * ei + ri * pr], axis=1)
    return x1, split(jnp.concatenate([er, ei], axis=1))


def stack(a, b):
    return tuple(jnp.concatenate(pair, axis=0) for pair in zip(a, b))


def invert(matrices):
    x1, e0 = zip(*[begin(*m) for m in matrices])
    e1 = [split(product(e, e)) for e in e0]
    both = [product(stack(split(x), e), e) for x, e in zip(x1, e1)]
    x2 = [x + b[:M] for x, b in zip(x1, both)]
    return [x + product(split(x), split(b[M:])) for x, b in zip(x2, both)]


def kernel(
    d_hbm, first_hbm, twiddle_hbm, second_hbm, out_hbm,
    d_ref, first_ref, twiddle_ref, second_ref, out_ref,
    mat, s0, s1, r0, r1, t0, t1, v0, v1, up_h, up_l, ssem, rsem, dsem, csem, osem,
):
    qx = lax.axis_index("qx")
    qy = lax.axis_index("qy")
    me = qx * SIZE_Y + qy

    def fetch(x):
        return pltpu.make_async_copy(d_hbm.at[:, x], d_ref.at[:, x], dsem.at[x])

    for x in range(LOCAL_X):
        fetch(x).start()
    constants = [
        pltpu.make_async_copy(first_hbm, first_ref, csem.at[0]),
        pltpu.make_async_copy(twiddle_hbm, twiddle_ref, csem.at[1]),
        pltpu.make_async_copy(second_hbm, second_ref, csem.at[2]),
    ]
    for copy in constants:
        copy.start()

    barrier = pltpu.get_barrier_semaphore()

    def greet(o):
        other = jnp.bitwise_xor(me, o)
        pl.semaphore_signal(
            barrier, inc=1, device_id=(other >> 3, other & 7), device_id_type=MESH
        )

    for o in range(1, 4):
        greet(o)

    def invert_some(x, carry):
        fetch(x).wait()
        lane = lax.broadcasted_iota(jnp.int32, (LOCAL_Y, L), 1)
        base = x * (LOCAL_Y * M)
        for part in range(2):
            for i in range(M):
                tile, off = divmod(i * M, L)
                row = d_ref[part, x, :, tile * L : (tile + 1) * L]
                if off:
                    row = pltpu.roll(row, L - off, 1)
                if off + M > L:
                    after = d_ref[part, x, :, (tile + 1) * L : (tile + 2) * L]
                    row = jnp.where(lane < L - off, row, pltpu.roll(after, L - off, 1))
                mat[part, pl.ds(base + i, LOCAL_Y, stride=M), :] = row
        for o in range(31):
            greet(4 + x * 31 + o)
        rows = [pl.ds(pl.multiple_of(base + k * M, M), M) for k in range(LOCAL_Y)]
        results = invert([(mat[0, r, :], mat[1, r, :]) for r in rows])
        for r, result in zip(rows, results):
            mat[0, r, :] = result[:, :L]
            mat[1, r, :] = result[:, L:]
        return carry

    lax.fori_loop(0, LOCAL_X, invert_some, 0)

    sends = (s0, s1)
    lands = (r0, r1)
    outs = (t0, t1)
    backs = (v0, v1)

    def exchange(src, dst, c, phase):
        used = pl.ds(0, USED[c])
        own = pltpu.make_async_copy(src.at[me, used], dst.at[me, used], rsem.at[phase, c])
        own.start()

        def send(o, carry):
            z, x, y, h = qx >> 2, (qx & 3) + (o & 3), (qy >> 1) + (o >> 2), qy & 1
            for n in range(8):
                k, core = n & 3, n >> 2
                tx = (((z + k) & 3) << 2) | ((x + k) & 3)
                ty = (((y + k) & 3) << 1) | (h ^ core)
                target = (tx << 3) | ty

                def start():
                    pltpu.make_async_remote_copy(
                        src_ref=src.at[target, used],
                        dst_ref=dst.at[me, used],
                        send_sem=ssem.at[phase, c],
                        recv_sem=rsem.at[phase, c],
                        device_id=(tx, ty),
                        device_id_type=MESH,
                    ).start()

                if n == 0:
                    pl.when(target != me)(start)
                else:
                    start()
            return carry

        lax.fori_loop(0, NDEV // 8, send, 0)

    def arrived(dst, c, phase):
        whole = dst.at[:, pl.ds(0, USED[c])]
        pltpu.make_async_copy(whole, whole, rsem.at[phase, c]).wait()

    def sent(src, c, phase):
        whole = src.at[pl.ds(0, NDEV - 1), pl.ds(0, USED[c])]
        pltpu.make_async_copy(whole, whole, ssem.at[phase, c]).wait()

    def flat(ref, c):
        return ref.reshape(NDEV * PITCH[c], L)

    def pack(c, part, u, v, first_row):
        block = jnp.concatenate(
            [
                mat[part, pl.ds(16 * u + 4 * g + v, Q, stride=M), :]
                for g in range(4)
            ],
            axis=0,
        ).T
        for w in range(3):
            lo, hi = max(0, w * L - v * M), min(M, (w + 1) * L - v * M)
            if lo >= hi:
                continue
            row = 3 * u + w
            c = 0 if row < ROWS[0] else 1
            local = part * ROWS[c] + row - (0 if c == 0 else ROWS[0])
            target = v * M + lo - w * L
            flat(sends[c], c)[pl.ds(target * PITCH[c] + local, hi - lo, stride=PITCH[c]), :] = block[lo:hi]

    for u in range(6):
        for v in range(4):
            for part in range(2):
                pack(0, part, u, v, 0)
        if u == 2:
            pl.semaphore_wait(barrier, NDEV - 1)
            exchange(s0, r0, 0, 0)
    exchange(s1, r1, 1, 0)

    def stage_one(c, pair):
        src = flat(lands[c], c)
        cols = []
        for row in (2 * pair, 2 * pair + 1):
            cols.append(
                jnp.concatenate(
                    [src[pl.ds(part * ROWS[c] + row, NDEV, stride=PITCH[c]), :] for part in range(2)],
                    axis=0,
                )
            )
        high, low = split(jnp.concatenate(cols, axis=1))
        table = first_ref[...]
        both = dot(table, high)
        total = both[: 2 * L] + both[2 * L :] + dot(table[: 2 * L], low)
        tr, ti = twiddle_ref[0], twiddle_ref[1]
        for k in range(2):
            real, imag = total[:L, k * L : (k + 1) * L], total[L:, k * L : (k + 1) * L]
            yield jnp.concatenate([real * tr - imag * ti, real * ti + imag * tr], axis=1)

    def stage_two(c0, n):
        high, low = up_h[c0], up_l[c0]
        table = second_ref[...]
        both = dot(table, high, 1)
        return both[: 2 * L] + both[2 * L :] + dot(table[: 2 * L], low, 1)

    def transform(c):
        for pair in range(4):
            for k, rows in enumerate(stage_one(c, pair)):
                high, low = split(rows)
                row = 2 * pair + k
                for c0 in range(4):
                    up_h[c0, row * Q : (row + 1) * Q, :] = high[c0 * Q : (c0 + 1) * Q]
                    up_l[c0, row * Q : (row + 1) * Q, :] = low[c0 * Q : (c0 + 1) * Q]
        dst = flat(outs[c], c)
        for c0 in range(4):
            result = stage_two(c0, 0)
            for part in range(2):
                for g in range(4):
                    for jx in range(4):
                        r = part * L + g * Q + jx * 8
                        for quad in range(2):
                            dst[
                                pl.ds((4 * jx + c0) * 8 * PITCH[c] + part * 8 + g * 2 + quad, 8, stride=PITCH[c]), :
                            ] = result[r : r + 8, quad * L : (quad + 1) * L]
        if c == 0:
            return
        for k, rows in enumerate(stage_one(c, 4)):
            high, low = split(rows)
            for c0 in range(4):
                at = c0 * 2 * Q + k * Q
                up_h[0, at : at + Q, :] = high[c0 * Q : (c0 + 1) * Q]
                up_l[0, at : at + Q, :] = low[c0 * Q : (c0 + 1) * Q]
        result = stage_two(0, 0)
        lane = lax.broadcasted_iota(jnp.int32, (8, L), 1)
        for c0 in range(4):
            col = c0 // 2 * L
            for part in range(2):
                for gh in range(2):
                    for jx in range(4):
                        r = part * L + gh * 2 * Q + jx * 8
                        one = result[r : r + 8, col : col + L]
                        two = result[r + Q : r + Q + 8, col : col + L]
                        if c0 % 2 == 0:
                            row = jnp.where(lane < 64, one, pltpu.roll(two, 64, 1))
                        else:
                            row = jnp.where(lane < 64, pltpu.roll(one, 64, 1), two)
                        dst[
                            pl.ds((4 * jx + c0) * 8 * PITCH[c] + 16 + part * 2 + gh, 8, stride=PITCH[c]), :
                        ] = row

    def write(tile, tiles):
        part = pl.ds(tile * L, tiles * L)
        return pltpu.make_async_copy(out_ref.at[:, :, :, part], out_hbm.at[:, :, :, part], osem.at[tile // 24])

    def place(part, g, row, block):
        tile = 12 * (row // 3) + 3 * g + row % 3
        out_ref[part, :, :, tile * L : (tile + 1) * L] = block.reshape(LOCAL_X, LOCAL_Y, L)

    def finish(c, quad):
        src = flat(backs[c], c)
        for part in range(2):
            for g in range(4):
                block = src[pl.ds(part * 8 + g * 2 + quad, NDEV, stride=PITCH[c]), :].T
                for k in range(4):
                    place(part, g, 8 * c + 4 * quad + k, block[k * Q : (k + 1) * Q])

    def finish_last():
        src = flat(v1, 1)
        for part in range(2):
            for gh in range(2):
                block = src[pl.ds(16 + part * 2 + gh, NDEV, stride=PITCH[1]), :].T
                for gl in range(2):
                    for k in range(2):
                        at = (2 * gl + k) * Q
                        place(part, 2 * gh + gl, 16 + k, block[at : at + Q])

    for copy in constants:
        copy.wait()
    for c in range(2):
        arrived(lands[c], c, 0)
        transform(c)
        exchange(outs[c], backs[c], c, 1)
    arrived(v0, 0, 1)
    finish(0, 0)
    finish(0, 1)
    write(0, 24).start()
    arrived(v1, 1, 1)
    finish(1, 0)
    write(24, 24).start()
    finish(1, 1)
    finish_last()
    write(48, 24).start()
    for c in range(2):
        sent(sends[c], c, 0)
        sent(outs[c], c, 1)
    for n in range(3):
        write(24 * n, 24).wait()


def per_device(dynamical):
    anywhere = pl.BlockSpec(memory_space=pl.ANY)
    constants = tables()
    buffers = [pltpu.VMEM((NDEV, p, L), F32) for p in PITCH]
    return pl.pallas_call(
        kernel,
        out_shape=jax.ShapeDtypeStruct(dynamical.shape, F32),
        in_specs=[anywhere] * 4,
        out_specs=anywhere,
        scratch_shapes=[
            pltpu.VMEM(dynamical.shape, F32),
            *[pltpu.VMEM(table.shape, table.dtype) for table in constants],
            pltpu.VMEM(dynamical.shape, F32),
            pltpu.VMEM((2, Q * M, L), F32),
            *buffers, *buffers, *buffers, *buffers,
            pltpu.VMEM((4, 2 * L, 2 * L), BF16),
            pltpu.VMEM((4, 2 * L, 2 * L), BF16),
            pltpu.SemaphoreType.DMA((2, 2)),
            pltpu.SemaphoreType.DMA((2, 2)),
            pltpu.SemaphoreType.DMA((LOCAL_X,)),
            pltpu.SemaphoreType.DMA((3,)),
            pltpu.SemaphoreType.DMA((3,)),
        ],
        compiler_params=pltpu.CompilerParams(
            collective_id=0, has_side_effects=True, vmem_limit_bytes=48 << 20
        ),
    )(dynamical, *constants)


def solution(mesh):
    return jax.shard_map(
        per_device,
        mesh=mesh,
        in_specs=(P(None, "qx", "qy", None),),
        out_specs=P(None, "qx", "qy", None),
        check_vma=False,
    )
```

```python
import functools

import jax
import jax.numpy as jnp
import ml_dtypes
import numpy as np
from jax import lax
from jax.experimental import pallas as pl
from jax.experimental.pallas import tpu as pltpu
from jax.sharding import PartitionSpec as P

M = 96
ETA = 0.25
NDEV = 128
SIZE_X, SIZE_Y = 16, 8
LOCAL_X, LOCAL_Y = 4, 8
Q = LOCAL_X * LOCAL_Y
L = 128
ROWS = (8, 10)
PITCH = (16, 24)
USED = (16, 20)
MESH = pl.DeviceIdType.MESH
F32 = jnp.float32
BF16 = jnp.bfloat16


def split_table(table):
    high = table.astype(ml_dtypes.bfloat16)
    low = (table - high.astype(np.float64)).astype(ml_dtypes.bfloat16)
    return high, low


def embed_table(angle):
    cosine, sine = np.cos(angle), np.sin(angle)
    return np.block([[cosine, -sine], [sine, cosine]])


def tables():
    ax, ay = np.divmod(np.arange(NDEV), SIZE_Y)
    turns = (ax[:, None] * ax[None, :] % 16) / 16 + (ay[:, None] * ay[None, :] % 8) / 8
    first = np.concatenate(split_table(embed_table(2 * np.pi * turns)), axis=0)
    lane = np.arange(L)
    bx, by = lane % Q // LOCAL_Y, lane % LOCAL_Y
    turns = (ax[:, None] * bx[None, :] + ay[:, None] * by[None, :]) / 64
    twiddle = np.stack([np.cos(2 * np.pi * turns), np.sin(2 * np.pi * turns)]) / 64
    turns = (bx[:, None] * bx[None, :] % 4) / 4 + (by[:, None] * by[None, :] % 8) / 8
    same = (lane[:, None] // Q) == (lane[None, :] // Q)
    angle = 2 * np.pi * turns
    cosine, sine = np.cos(angle) * same, np.sin(angle) * same
    second = np.concatenate(split_table(np.block([[cosine, -sine], [sine, cosine]])), axis=0)
    return first, twiddle.astype(np.float32), second


def split(value):
    high = value.astype(BF16)
    low = (value - high.astype(F32)).astype(BF16)
    return high, low


def dot(a, b, contract=0):
    return lax.dot_general(a, b, (((1,), (contract,)), ((), ())), preferred_element_type=F32)


def embed(part):
    zeros = jnp.zeros((L - M, 2 * L), part.dtype)
    real, imag = part[:, :L], part[:, L:]
    return jnp.concatenate(
        [part, zeros, jnp.concatenate([-imag, real], axis=1), zeros], axis=0
    )


def product(left, right):
    n = left[0].shape[0]
    both = dot(jnp.concatenate(left, axis=0), embed(right[0]))
    return both[:n] + both[n:] + dot(left[0], embed(right[1]))


def begin(real, imag):
    row = lax.broadcasted_iota(jnp.int32, (M, L), 0)
    col = lax.broadcasted_iota(jnp.int32, (M, L), 1)
    eye = row == col
    off = (col < M) & (row != col)
    diag = jnp.where(eye, real, 0.0)

    def start(d):
        denom = d * d + ETA * ETA
        return d / denom, -ETA / denom

    cr, ci = start(jnp.sum(diag, axis=0, keepdims=True))
    rr, ri = start(jnp.sum(diag, axis=1, keepdims=True))
    er = jnp.where(off, imag * ci - real * cr, 0.0)
    ei = jnp.where(off, -(real * ci + imag * cr), 0.0)
    pr = jnp.where(eye, 1.0, er)
    x1 = jnp.concatenate([rr * pr - ri * ei, rr * ei + ri * pr], axis=1)
    return x1, split(jnp.concatenate([er, ei], axis=1))


def stack(a, b):
    return tuple(jnp.concatenate(pair, axis=0) for pair in zip(a, b))


def invert(matrices):
    x1, e0 = zip(*[begin(*m) for m in matrices])
    e1 = [split(product(e, e)) for e in e0]
    both = [product(stack(split(x), e), e) for x, e in zip(x1, e1)]
    x2 = [x + b[:M] for x, b in zip(x1, both)]
    return [x + product(split(x), split(b[M:])) for x, b in zip(x2, both)]


def kernel(
    d_hbm, first_hbm, twiddle_hbm, second_hbm, out_ref,
    d_ref, first_ref, twiddle_ref, second_ref,
    mat, s0, s1, r0, r1, t0, t1, v0, v1, up_h, up_l, ssem, rsem, dsem, csem, both_sem,
):
    qx = lax.axis_index("qx")
    qy = lax.axis_index("qy")
    me = qx * SIZE_Y + qy

    def fetch(x):
        return pltpu.make_async_copy(d_hbm.at[:, x], d_ref.at[:, x], dsem.at[x])

    for x in range(LOCAL_X):
        fetch(x).start()
    constants = [
        pltpu.make_async_copy(first_hbm, first_ref, csem.at[0]),
        pltpu.make_async_copy(twiddle_hbm, twiddle_ref, csem.at[1]),
        pltpu.make_async_copy(second_hbm, second_ref, csem.at[2]),
    ]
    for copy in constants:
        copy.start()

    barrier = pltpu.get_barrier_semaphore()

    def hops(o):
        return sum((0, 1, 2, 1)[o >> n & 3] for n in (1, 3, 5))

    for o in [*sorted(range(2, NDEV, 2), key=hops, reverse=True), 1]:
        other = jnp.bitwise_xor(me, o)
        pl.semaphore_signal(
            barrier, inc=1, device_id=(other >> 3, other & 7), device_id_type=MESH
        )

    def all_entered():
        pl.semaphore_wait(barrier, NDEV // 2)
        pl.semaphore_signal(
            both_sem, inc=1, device_id=(qx, jnp.bitwise_xor(qy, 1)), device_id_type=MESH
        )
        pl.semaphore_wait(both_sem, 1)

    def invert_some(x, carry):
        fetch(x).wait()
        lane = lax.broadcasted_iota(jnp.int32, (LOCAL_Y, L), 1)
        base = x * (LOCAL_Y * M)
        for part in range(2):
            for i in range(M):
                tile, off = divmod(i * M, L)
                row = d_ref[part, x, :, tile * L : (tile + 1) * L]
                if off:
                    row = pltpu.roll(row, L - off, 1)
                if off + M > L:
                    after = d_ref[part, x, :, (tile + 1) * L : (tile + 2) * L]
                    row = jnp.where(lane < L - off, row, pltpu.roll(after, L - off, 1))
                mat[part, pl.ds(base + i, LOCAL_Y, stride=M), :] = row
        rows = [pl.ds(pl.multiple_of(base + k * M, M), M) for k in range(LOCAL_Y)]
        results = invert([(mat[0, r, :], mat[1, r, :]) for r in rows])
        for r, result in zip(rows, results):
            mat[0, r, :] = result[:, :L]
            mat[1, r, :] = result[:, L:]
        return carry

    lax.fori_loop(0, LOCAL_X, invert_some, 0)

    sends = (s0, s1)
    lands = (r0, r1)
    outs = (t0, t1)
    backs = (v0, v1)

    def exchange(src, dst, c, phase):
        used = pl.ds(0, USED[c])
        own = pltpu.make_async_copy(src.at[me, used], dst.at[me, used], rsem.at[phase, c])
        own.start()

        def send(o, carry):
            z, x, y, h = qx >> 2, (qx & 3) + (o & 3), (qy >> 1) + (o >> 2), qy & 1
            for n in range(8):
                k, core = n & 3, n >> 2
                tx = (((z + k) & 3) << 2) | ((x + k) & 3)
                ty = (((y + k) & 3) << 1) | (h ^ core)
                target = (tx << 3) | ty

                def start():
                    pltpu.make_async_remote_copy(
                        src_ref=src.at[target, used],
                        dst_ref=dst.at[me, used],
                        send_sem=ssem.at[phase, c],
                        recv_sem=rsem.at[phase, c],
                        device_id=(tx, ty),
                        device_id_type=MESH,
                    ).start()

                if n == 0:
                    pl.when(target != me)(start)
                else:
                    start()
            return carry

        lax.fori_loop(0, NDEV // 8, send, 0)

    def arrived(dst, c, phase):
        whole = dst.at[:, pl.ds(0, USED[c])]
        pltpu.make_async_copy(whole, whole, rsem.at[phase, c]).wait()

    def sent(src, c, phase):
        whole = src.at[pl.ds(0, NDEV - 1), pl.ds(0, USED[c])]
        pltpu.make_async_copy(whole, whole, ssem.at[phase, c]).wait()

    def flat(ref, c):
        return ref.reshape(NDEV * PITCH[c], L)

    def pack(c, part, u, v, first_row):
        block = jnp.concatenate(
            [
                mat[part, pl.ds(16 * u + 4 * g + v, Q, stride=M), :]
                for g in range(4)
            ],
            axis=0,
        ).T
        for w in range(3):
            lo, hi = max(0, w * L - v * M), min(M, (w + 1) * L - v * M)
            if lo >= hi:
                continue
            row = 3 * u + w
            c = 0 if row < ROWS[0] else 1
            local = part * ROWS[c] + row - (0 if c == 0 else ROWS[0])
            target = v * M + lo - w * L
            flat(sends[c], c)[pl.ds(target * PITCH[c] + local, hi - lo, stride=PITCH[c]), :] = block[lo:hi]

    for u in range(6):
        for v in range(4):
            for part in range(2):
                pack(0, part, u, v, 0)
        if u == 2:
            all_entered()
            exchange(s0, r0, 0, 0)
    exchange(s1, r1, 1, 0)

    def stage_one(c, pair):
        src = flat(lands[c], c)
        cols = []
        for row in (2 * pair, 2 * pair + 1):
            cols.append(
                jnp.concatenate(
                    [src[pl.ds(part * ROWS[c] + row, NDEV, stride=PITCH[c]), :] for part in range(2)],
                    axis=0,
                )
            )
        high, low = split(jnp.concatenate(cols, axis=1))
        table = first_ref[...]
        both = dot(table, high)
        total = both[: 2 * L] + both[2 * L :] + dot(table[: 2 * L], low)
        tr, ti = twiddle_ref[0], twiddle_ref[1]
        for k in range(2):
            real, imag = total[:L, k * L : (k + 1) * L], total[L:, k * L : (k + 1) * L]
            yield jnp.concatenate([real * tr - imag * ti, real * ti + imag * tr], axis=1)

    def stage_two(c0, n):
        high, low = up_h[c0], up_l[c0]
        table = second_ref[...]
        both = dot(table, high, 1)
        return both[: 2 * L] + both[2 * L :] + dot(table[: 2 * L], low, 1)

    def transform(c):
        for pair in range(4):
            for k, rows in enumerate(stage_one(c, pair)):
                high, low = split(rows)
                row = 2 * pair + k
                for c0 in range(4):
                    up_h[c0, row * Q : (row + 1) * Q, :] = high[c0 * Q : (c0 + 1) * Q]
                    up_l[c0, row * Q : (row + 1) * Q, :] = low[c0 * Q : (c0 + 1) * Q]
        dst = flat(outs[c], c)
        for c0 in range(4):
            result = stage_two(c0, 0)
            for part in range(2):
                for g in range(4):
                    for jx in range(4):
                        r = part * L + g * Q + jx * 8
                        for quad in range(2):
                            dst[
                                pl.ds((4 * jx + c0) * 8 * PITCH[c] + part * 8 + g * 2 + quad, 8, stride=PITCH[c]), :
                            ] = result[r : r + 8, quad * L : (quad + 1) * L]
        if c == 0:
            return
        for k, rows in enumerate(stage_one(c, 4)):
            high, low = split(rows)
            for c0 in range(4):
                at = c0 * 2 * Q + k * Q
                up_h[0, at : at + Q, :] = high[c0 * Q : (c0 + 1) * Q]
                up_l[0, at : at + Q, :] = low[c0 * Q : (c0 + 1) * Q]
        result = stage_two(0, 0)
        lane = lax.broadcasted_iota(jnp.int32, (8, L), 1)
        for c0 in range(4):
            col = c0 // 2 * L
            for part in range(2):
                for gh in range(2):
                    for jx in range(4):
                        r = part * L + gh * 2 * Q + jx * 8
                        one = result[r : r + 8, col : col + L]
                        two = result[r + Q : r + Q + 8, col : col + L]
                        if c0 % 2 == 0:
                            row = jnp.where(lane < 64, one, pltpu.roll(two, 64, 1))
                        else:
                            row = jnp.where(lane < 64, pltpu.roll(one, 64, 1), two)
                        dst[
                            pl.ds((4 * jx + c0) * 8 * PITCH[c] + 16 + part * 2 + gh, 8, stride=PITCH[c]), :
                        ] = row

    def place(part, g, row, block):
        tile = 12 * (row // 3) + 3 * g + row % 3
        out_ref[part, :, :, tile * L : (tile + 1) * L] = block.reshape(LOCAL_X, LOCAL_Y, L)

    def finish(c, quad):
        src = flat(backs[c], c)
        for part in range(2):
            for g in range(4):
                block = src[pl.ds(part * 8 + g * 2 + quad, NDEV, stride=PITCH[c]), :].T
                for k in range(4):
                    place(part, g, 8 * c + 4 * quad + k, block[k * Q : (k + 1) * Q])

    def finish_last():
        src = flat(v1, 1)
        for part in range(2):
            for gh in range(2):
                block = src[pl.ds(16 + part * 2 + gh, NDEV, stride=PITCH[1]), :].T
                for gl in range(2):
                    for k in range(2):
                        at = (2 * gl + k) * Q
                        place(part, 2 * gh + gl, 16 + k, block[at : at + Q])

    for copy in constants:
        copy.wait()
    for c in range(2):
        arrived(lands[c], c, 0)
        transform(c)
        exchange(outs[c], backs[c], c, 1)
    arrived(v0, 0, 1)
    finish(0, 0)
    finish(0, 1)
    arrived(v1, 1, 1)
    finish(1, 0)
    finish(1, 1)
    finish_last()
    for c in range(2):
        sent(sends[c], c, 0)
        sent(outs[c], c, 1)


def per_device(dynamical):
    constants = tables()
    operands = [
        pltpu.with_memory_space_constraint(operand, pltpu.HBM)
        for operand in (dynamical, *map(jnp.asarray, constants))
    ]
    buffers = [pltpu.VMEM((NDEV, p, L), F32) for p in PITCH]
    return pl.pallas_call(
        kernel,
        out_shape=pltpu.VMEM(dynamical.shape, F32),
        in_specs=[pl.BlockSpec(memory_space=pltpu.HBM)] * 4,
        out_specs=pl.BlockSpec(memory_space=pltpu.VMEM),
        scratch_shapes=[
            pltpu.VMEM(dynamical.shape, F32),
            *[pltpu.VMEM(table.shape, table.dtype) for table in constants],
            pltpu.VMEM((2, Q * M, L), F32),
            *buffers, *buffers, *buffers, *buffers,
            pltpu.VMEM((4, 2 * L, 2 * L), BF16),
            pltpu.VMEM((4, 2 * L, 2 * L), BF16),
            pltpu.SemaphoreType.DMA((2, 2)),
            pltpu.SemaphoreType.DMA((2, 2)),
            pltpu.SemaphoreType.DMA((LOCAL_X,)),
            pltpu.SemaphoreType.DMA((3,)),
            pltpu.SemaphoreType.REGULAR,
        ],
        compiler_params=pltpu.CompilerParams(
            collective_id=0, has_side_effects=True, vmem_limit_bytes=48 << 20
        ),
    )(*operands)


def solution(mesh):
    return jax.shard_map(
        per_device,
        mesh=mesh,
        in_specs=(P(None, "qx", "qy", None),),
        out_specs=P(None, "qx", "qy", None),
        check_vma=False,
    )
```

```python
import functools

import jax
import jax.numpy as jnp
import ml_dtypes
import numpy as np
from jax import lax
from jax.experimental import pallas as pl
from jax.experimental.pallas import tpu as pltpu
from jax.sharding import PartitionSpec as P

M = 96
ETA = 0.25
NDEV = 128
SIZE_X, SIZE_Y = 16, 8
LOCAL_X, LOCAL_Y = 4, 8
Q = LOCAL_X * LOCAL_Y
L = 128
HALF = Q // 2
GROUPS = L // HALF
USED = (18, 8, 10, 16, 20)
PITCH = (24, 8, 16, 16, 24)
MESH = pl.DeviceIdType.MESH
F32 = jnp.float32
BF16 = jnp.bfloat16


def split_table(table):
    high = table.astype(ml_dtypes.bfloat16)
    low = (table - high.astype(np.float64)).astype(ml_dtypes.bfloat16)
    return high, low


def embed_table(angle):
    cosine, sine = np.cos(angle), np.sin(angle)
    return np.block([[cosine, -sine], [sine, cosine]])


def tables():
    ax, ay = np.divmod(np.arange(NDEV), SIZE_Y)
    turns = (ax[:, None] * ax[None, :] % 16) / 16 + (ay[:, None] * ay[None, :] % 8) / 8
    first = np.concatenate(split_table(embed_table(2 * np.pi * turns)), axis=0)
    lane = np.arange(L)
    group, bl, by = lane // HALF, lane % HALF // LOCAL_Y, lane % LOCAL_Y
    turns = np.stack(
        [
            (ax[:, None] * (2 * bh + bl)[None, :] + ay[:, None] * by[None, :]) / 64
            for bh in range(2)
        ]
    )
    twiddle = np.stack([np.cos(2 * np.pi * turns), np.sin(2 * np.pi * turns)], axis=1) / 64
    same = group[:, None] == group[None, :]
    second = []
    for j0 in range(2):
        turns = (2 * bl + j0)[:, None] * bl[None, :] / 4 + (by[:, None] * by[None, :] % 8) / 8
        cosine, sine = np.cos(2 * np.pi * turns) * same, np.sin(2 * np.pi * turns) * same
        table = split_table(np.block([[cosine, -sine], [sine, cosine]]))
        second.append(np.concatenate(table, axis=0))
    return first, twiddle.astype(np.float32), np.stack(second)


def split(value):
    high = value.astype(BF16)
    low = (value - high.astype(F32)).astype(BF16)
    return high, low


def dot(a, b, contract=0):
    return lax.dot_general(a, b, (((1,), (contract,)), ((), ())), preferred_element_type=F32)


def embed(part):
    zeros = jnp.zeros((L - M, 2 * L), part.dtype)
    real, imag = part[:, :L], part[:, L:]
    return jnp.concatenate(
        [part, zeros, jnp.concatenate([-imag, real], axis=1), zeros], axis=0
    )


def product(left, right):
    n = left[0].shape[0]
    both = dot(jnp.concatenate(left, axis=0), embed(right[0]))
    return both[:n] + both[n:] + dot(left[0], embed(right[1]))


def begin(real, imag):
    row = lax.broadcasted_iota(jnp.int32, (M, L), 0)
    col = lax.broadcasted_iota(jnp.int32, (M, L), 1)
    eye = row == col
    off = (col < M) & (row != col)
    diag = jnp.where(eye, real, 0.0)

    def start(d):
        denom = d * d + ETA * ETA
        return d / denom, -ETA / denom

    cr, ci = start(jnp.sum(diag, axis=0, keepdims=True))
    rr, ri = start(jnp.sum(diag, axis=1, keepdims=True))
    er = jnp.where(off, imag * ci - real * cr, 0.0)
    ei = jnp.where(off, -(real * ci + imag * cr), 0.0)
    pr = jnp.where(eye, 1.0, er)
    x1 = jnp.concatenate([rr * pr - ri * ei, rr * ei + ri * pr], axis=1)
    return x1, split(jnp.concatenate([er, ei], axis=1))


def stack(a, b):
    return tuple(jnp.concatenate(pair, axis=0) for pair in zip(a, b))


def invert(matrices):
    x1, e0 = zip(*[begin(*m) for m in matrices])
    e1 = [split(product(e, e)) for e in e0]
    both = [product(stack(split(x), e), e) for x, e in zip(x1, e1)]
    x2 = [x + b[:M] for x, b in zip(x1, both)]
    return [x + product(split(x), split(b[M:])) for x, b in zip(x2, both)]


def kernel(
    d_hbm, first_hbm, twiddle_hbm, second_hbm, out_ref,
    d_ref, first_ref, twiddle_ref, second_ref,
    mat, s0, s1, s2, t0, t1, r0, r1, r2, v0, v1, up_h, up_l, ssem, rsem, dsem, csem, both_sem,
):
    qx = lax.axis_index("qx")
    qy = lax.axis_index("qy")
    me = qx * SIZE_Y + qy

    def fetch(x):
        return pltpu.make_async_copy(d_hbm.at[:, x], d_ref.at[:, x], dsem.at[x])

    for x in range(LOCAL_X):
        fetch(x).start()
    constants = [
        pltpu.make_async_copy(first_hbm, first_ref, csem.at[0]),
        pltpu.make_async_copy(twiddle_hbm, twiddle_ref, csem.at[1]),
        pltpu.make_async_copy(second_hbm, second_ref, csem.at[2]),
    ]
    for copy in constants:
        copy.start()

    barrier = pltpu.get_barrier_semaphore()

    def hops(o):
        return sum((0, 1, 2, 1)[o >> n & 3] for n in (1, 3, 5))

    for o in [*sorted(range(2, NDEV, 2), key=hops, reverse=True), 1]:
        other = jnp.bitwise_xor(me, o)
        pl.semaphore_signal(
            barrier, inc=1, device_id=(other >> 3, other & 7), device_id_type=MESH
        )

    def all_entered():
        pl.semaphore_wait(barrier, NDEV // 2)
        pl.semaphore_signal(
            both_sem, inc=1, device_id=(qx, jnp.bitwise_xor(qy, 1)), device_id_type=MESH
        )
        pl.semaphore_wait(both_sem, 1)

    def invert_some(x, carry):
        fetch(x).wait()
        lane = lax.broadcasted_iota(jnp.int32, (LOCAL_Y, L), 1)
        base = x * (LOCAL_Y * M)
        for part in range(2):
            for i in range(M):
                tile, off = divmod(i * M, L)
                row = d_ref[part, x, :, tile * L : (tile + 1) * L]
                if off:
                    row = pltpu.roll(row, L - off, 1)
                if off + M > L:
                    after = d_ref[part, x, :, (tile + 1) * L : (tile + 2) * L]
                    row = jnp.where(lane < L - off, row, pltpu.roll(after, L - off, 1))
                mat[part, pl.ds(base + i, LOCAL_Y, stride=M), :] = row
        rows = [pl.ds(pl.multiple_of(base + k * M, M), M) for k in range(LOCAL_Y)]
        results = invert([(mat[0, r, :], mat[1, r, :]) for r in rows])
        for r, result in zip(rows, results):
            mat[0, r, :] = result[:, :L]
            mat[1, r, :] = result[:, L:]
        return carry

    sources = (s0, s1, s2, t0, t1)
    places = (r0, r1, r2, v0, v1)

    def exchange(c):
        src, dst = sources[c], places[c]
        used = pl.ds(0, USED[c])
        own = pltpu.make_async_copy(src.at[me, used], dst.at[me, used], rsem.at[c])
        own.start()

        def send(o, carry):
            z, x, y, h = qx >> 2, (qx & 3) + (o & 3), (qy >> 1) + (o >> 2), qy & 1
            for n in range(8):
                k, core = n & 3, n >> 2
                tx = (((z + k) & 3) << 2) | ((x + k) & 3)
                ty = (((y + k) & 3) << 1) | (h ^ core)
                target = (tx << 3) | ty

                def start():
                    pltpu.make_async_remote_copy(
                        src_ref=src.at[target, used],
                        dst_ref=dst.at[me, used],
                        send_sem=ssem.at[c],
                        recv_sem=rsem.at[c],
                        device_id=(tx, ty),
                        device_id_type=MESH,
                    ).start()

                if n == 0:
                    pl.when(target != me)(start)
                else:
                    start()
            return carry

        lax.fori_loop(0, NDEV // 8, send, 0)

    def arrived(c):
        whole = places[c].at[:, pl.ds(0, USED[c])]
        pltpu.make_async_copy(whole, whole, rsem.at[c]).wait()

    def sent(c):
        whole = sources[c].at[pl.ds(0, NDEV - 1), pl.ds(0, USED[c])]
        pltpu.make_async_copy(whole, whole, ssem.at[c]).wait()

    def flat(ref, c):
        return ref.reshape(NDEV * PITCH[c], L)

    def pack(half, u):
        for v in range(4):
            for part in range(2):
                first = half * HALF * M + 4 * GROUPS * u + v
                block = jnp.concatenate(
                    [mat[part, pl.ds(first + 4 * g, HALF, stride=M), :] for g in range(GROUPS)], axis=0
                ).T
                for w in range(3):
                    lo, hi = max(0, w * L - v * M), min(M, (w + 1) * L - v * M)
                    if lo >= hi:
                        continue
                    row = 3 * u + w
                    if half == 0:
                        c, row = 0, part * 9 + row
                    elif row < 4:
                        c, row = 1, part * 4 + row
                    else:
                        c, row = 2, part * 5 + row - 4
                    at = (v * M + lo - w * L) * PITCH[c] + row
                    flat(sources[c], c)[pl.ds(at, hi - lo, stride=PITCH[c]), :] = block[lo:hi]

    def stage_one(row):
        c, first, count = (1, row, 4) if row < 4 else (2, row - 4, 5)
        cols = []
        for src, at, step in ((0, row, 9), (c, first, count)):
            ref = flat(places[src], src)
            cols.append(
                jnp.concatenate(
                    [ref[pl.ds(part * step + at, NDEV, stride=PITCH[src]), :] for part in range(2)], axis=0
                )
            )
        high, low = split(jnp.concatenate(cols, axis=1))
        table = first_ref[...]
        both = dot(table, high)
        total = both[: 2 * L] + both[2 * L :] + dot(table[: 2 * L], low)
        turned = []
        for bh in range(2):
            real, imag = total[:L, bh * L : (bh + 1) * L], total[L:, bh * L : (bh + 1) * L]
            tr, ti = twiddle_ref[bh, 0], twiddle_ref[bh, 1]
            turned.append(jnp.concatenate([real * tr - imag * ti, real * ti + imag * tr], axis=1))
        return turned[0] + turned[1], turned[0] - turned[1]

    def keep(row, at, pitch):
        for j0, value in enumerate(stage_one(row)):
            high, low = split(value)
            for c0 in range(4):
                rows = slice(c0 * pitch + at, c0 * pitch + at + Q)
                up_h[j0, rows, :] = high[c0 * Q : (c0 + 1) * Q]
                up_l[j0, rows, :] = low[c0 * Q : (c0 + 1) * Q]

    def stage_two(j0, rows):
        table = second_ref[j0]
        both = dot(table, up_h[j0, rows, :], 1)
        return both[: 2 * L] + both[2 * L :] + dot(table[: 2 * L], up_l[j0, rows, :], 1)

    def put(c, jx, c0, row, value):
        at = (4 * jx + c0) * LOCAL_Y * PITCH[c] + row
        flat(sources[c], c)[pl.ds(at, LOCAL_Y, stride=PITCH[c]), :] = value

    def transform(n):
        c = 3 + n
        for k in range(4):
            keep(4 * n + k, k * Q, L)
        for j0 in range(2):
            for pair in range(2):
                result = stage_two(j0, slice(pair * 2 * L, (pair + 1) * 2 * L))
                for part in range(2):
                    for g in range(GROUPS):
                        for j1 in range(2):
                            r = part * L + g * HALF + j1 * LOCAL_Y
                            for k in range(2):
                                put(
                                    c, 2 * j1 + j0, 2 * pair + k, part * GROUPS + g,
                                    result[r : r + LOCAL_Y, k * L : (k + 1) * L],
                                )
        if n == 0:
            return
        keep(8, 0, Q)
        lane = lax.broadcasted_iota(jnp.int32, (LOCAL_Y, L), 1)
        for j0 in range(2):
            result = stage_two(j0, slice(0, L))
            for part in range(2):
                for gh in range(2):
                    for j1 in range(2):
                        r = part * L + gh * 4 * HALF + j1 * LOCAL_Y
                        parts = [result[r + gl * HALF : r + gl * HALF + LOCAL_Y] for gl in range(4)]
                        for c0 in range(4):
                            row = parts[c0]
                            for gl in range(4):
                                if gl != c0:
                                    moved = pltpu.roll(parts[gl], (gl - c0) % 4 * Q, 1)
                                    row = jnp.where(lane // Q == gl, moved, row)
                            put(c, 2 * j1 + j0, c0, 2 * GROUPS + part * 2 + gh, row)

    def place(part, g, row, block):
        tile = 24 * (row // 3) + 3 * g + row % 3
        out_ref[part, :, :, tile * L : (tile + 1) * L] = block.reshape(LOCAL_X, LOCAL_Y, L)

    def finish(n):
        c = 3 + n
        src = flat(places[c], c)
        for part in range(2):
            for g in range(GROUPS):
                block = src[pl.ds(part * GROUPS + g, NDEV, stride=PITCH[c]), :].T
                for k in range(4):
                    place(part, g, 4 * n + k, block[k * Q : (k + 1) * Q])
            if n == 1:
                for gh in range(2):
                    block = src[pl.ds(2 * GROUPS + part * 2 + gh, NDEV, stride=PITCH[c]), :].T
                    for gl in range(4):
                        place(part, 4 * gh + gl, 8, block[gl * Q : (gl + 1) * Q])

    lax.fori_loop(0, LOCAL_X // 2, invert_some, 0)
    for u in range(3):
        pack(0, u)
    all_entered()
    exchange(0)
    lax.fori_loop(LOCAL_X // 2, LOCAL_X, invert_some, 0)
    pack(1, 0)
    pack(1, 1)
    exchange(1)
    pack(1, 2)
    exchange(2)
    for copy in constants:
        copy.wait()
    arrived(0)
    for n in range(2):
        arrived(1 + n)
        transform(n)
        exchange(3 + n)
    for n in range(2):
        arrived(3 + n)
        finish(n)
    for c in range(5):
        sent(c)


def per_device(dynamical):
    constants = tables()
    operands = [
        pltpu.with_memory_space_constraint(operand, pltpu.HBM)
        for operand in (dynamical, *map(jnp.asarray, constants))
    ]
    buffers = [pltpu.VMEM((NDEV, p, L), F32) for p in PITCH]
    return pl.pallas_call(
        kernel,
        out_shape=pltpu.VMEM(dynamical.shape, F32),
        in_specs=[pl.BlockSpec(memory_space=pltpu.HBM)] * 4,
        out_specs=pl.BlockSpec(memory_space=pltpu.VMEM),
        scratch_shapes=[
            pltpu.VMEM(dynamical.shape, F32),
            *[pltpu.VMEM(table.shape, table.dtype) for table in constants],
            pltpu.VMEM((2, Q * M, L), F32),
            *buffers, *buffers,
            pltpu.VMEM((2, 4 * L, 2 * L), BF16),
            pltpu.VMEM((2, 4 * L, 2 * L), BF16),
            pltpu.SemaphoreType.DMA((5,)),
            pltpu.SemaphoreType.DMA((5,)),
            pltpu.SemaphoreType.DMA((LOCAL_X,)),
            pltpu.SemaphoreType.DMA((3,)),
            pltpu.SemaphoreType.REGULAR,
        ],
        compiler_params=pltpu.CompilerParams(
            collective_id=0, has_side_effects=True, vmem_limit_bytes=48 << 20
        ),
    )(*operands)


def solution(mesh):
    return jax.shard_map(
        per_device,
        mesh=mesh,
        in_specs=(P(None, "qx", "qy", None),),
        out_specs=P(None, "qx", "qy", None),
        check_vma=False,
    )
```

```python
import functools

import jax
import jax.numpy as jnp
import ml_dtypes
import numpy as np
from jax import lax
from jax.experimental import pallas as pl
from jax.experimental.pallas import tpu as pltpu
from jax.sharding import PartitionSpec as P

M = 96
ETA = 0.25
NDEV = 128
SIZE_X, SIZE_Y = 16, 8
LOCAL_X, LOCAL_Y = 4, 8
Q = LOCAL_X * LOCAL_Y
L = 128
HALF = Q // 2
GROUPS = L // HALF
USED = (18, 8, 10, 16, 20)
PITCH = (24, 8, 16, 16, 24)
MESH = pl.DeviceIdType.MESH
F32 = jnp.float32
BF16 = jnp.bfloat16


def split_table(table):
    high = table.astype(ml_dtypes.bfloat16)
    low = (table - high.astype(np.float64)).astype(ml_dtypes.bfloat16)
    return high, low


def embed_table(angle):
    cosine, sine = np.cos(angle), np.sin(angle)
    return np.block([[cosine, -sine], [sine, cosine]])


def tables():
    ax, ay = np.divmod(np.arange(NDEV), SIZE_Y)
    turns = (ax[:, None] * ax[None, :] % 16) / 16 + (ay[:, None] * ay[None, :] % 8) / 8
    first = np.concatenate(split_table(embed_table(2 * np.pi * turns)), axis=0)
    lane = np.arange(L)
    group, bl, by = lane // HALF, lane % HALF // LOCAL_Y, lane % LOCAL_Y
    turns = np.stack(
        [
            (ax[:, None] * (2 * bh + bl)[None, :] + ay[:, None] * by[None, :]) / 64
            for bh in range(2)
        ]
    )
    twiddle = np.stack([np.cos(2 * np.pi * turns), np.sin(2 * np.pi * turns)], axis=1) / 64
    same = group[:, None] == group[None, :]
    second = []
    for j0 in range(2):
        turns = (2 * bl + j0)[:, None] * bl[None, :] / 4 + (by[:, None] * by[None, :] % 8) / 8
        cosine, sine = np.cos(2 * np.pi * turns) * same, np.sin(2 * np.pi * turns) * same
        table = split_table(np.block([[cosine, -sine], [sine, cosine]]))
        second.append(np.concatenate(table, axis=0))
    return first, twiddle.astype(np.float32), np.stack(second)


def split(value):
    high = value.astype(BF16)
    low = (value - high.astype(F32)).astype(BF16)
    return high, low


def dot(a, b, contract=0):
    return lax.dot_general(a, b, (((1,), (contract,)), ((), ())), preferred_element_type=F32)


def embed(part):
    zeros = jnp.zeros((L - M, 2 * L), part.dtype)
    real, imag = part[:, :L], part[:, L:]
    return jnp.concatenate(
        [part, zeros, jnp.concatenate([-imag, real], axis=1), zeros], axis=0
    )


def product(left, right):
    n = left[0].shape[0]
    both = dot(jnp.concatenate(left, axis=0), embed(right[0]))
    return both[:n] + both[n:] + dot(left[0], embed(right[1]))


def begin(real, imag):
    row = lax.broadcasted_iota(jnp.int32, (M, L), 0)
    col = lax.broadcasted_iota(jnp.int32, (M, L), 1)
    eye = row == col
    off = (col < M) & (row != col)
    diag = jnp.where(eye, real, 0.0)

    def start(d):
        denom = d * d + ETA * ETA
        return d / denom, -ETA / denom

    cr, ci = start(jnp.sum(diag, axis=0, keepdims=True))
    rr, ri = start(jnp.sum(diag, axis=1, keepdims=True))
    er = jnp.where(off, imag * ci - real * cr, 0.0)
    ei = jnp.where(off, -(real * ci + imag * cr), 0.0)
    pr = jnp.where(eye, 1.0, er)
    x1 = jnp.concatenate([rr * pr - ri * ei, rr * ei + ri * pr], axis=1)
    return x1, split(jnp.concatenate([er, ei], axis=1))


def stack(a, b):
    return tuple(jnp.concatenate(pair, axis=0) for pair in zip(a, b))


def invert(matrices):
    x1, e0 = zip(*[begin(*m) for m in matrices])
    e1 = [split(product(e, e)) for e in e0]
    both = [product(stack(split(x), e), e) for x, e in zip(x1, e1)]
    x2 = [x + b[:M] for x, b in zip(x1, both)]
    return [x + product(split(x), split(b[M:])) for x, b in zip(x2, both)]


def kernel(
    d_hbm, first_hbm, twiddle_hbm, second_hbm, out_ref,
    d_ref, first_ref, twiddle_ref, second_ref,
    mat, s0, s1, s2, t0, t1, r0, r1, r2, v0, v1, up_h, up_l, ssem, rsem, dsem, csem, both_sem,
):
    qx = lax.axis_index("qx")
    qy = lax.axis_index("qy")
    me = qx * SIZE_Y + qy

    def fetch(x):
        return pltpu.make_async_copy(d_hbm.at[:, x], d_ref.at[:, x], dsem.at[x])

    for x in range(LOCAL_X):
        fetch(x).start()
    constants = [
        pltpu.make_async_copy(first_hbm, first_ref, csem.at[0]),
        pltpu.make_async_copy(twiddle_hbm, twiddle_ref, csem.at[1]),
        pltpu.make_async_copy(second_hbm, second_ref, csem.at[2]),
    ]
    for copy in constants:
        copy.start()

    barrier = pltpu.get_barrier_semaphore()

    def hops(o):
        return sum((0, 1, 2, 1)[o >> n & 3] for n in (1, 3, 5))

    for o in [*sorted(range(2, NDEV, 2), key=hops, reverse=True), 1]:
        other = jnp.bitwise_xor(me, o)
        pl.semaphore_signal(
            barrier, inc=1, device_id=(other >> 3, other & 7), device_id_type=MESH
        )

    def all_entered():
        pl.semaphore_wait(barrier, NDEV // 2)
        pl.semaphore_signal(
            both_sem, inc=1, device_id=(qx, jnp.bitwise_xor(qy, 1)), device_id_type=MESH
        )
        pl.semaphore_wait(both_sem, 1)

    def invert_some(x, carry):
        fetch(x).wait()
        lane = lax.broadcasted_iota(jnp.int32, (LOCAL_Y, L), 1)
        base = x * (LOCAL_Y * M)
        for part in range(2):
            for i in range(M):
                tile, off = divmod(i * M, L)
                row = d_ref[part, x, :, tile * L : (tile + 1) * L]
                if off:
                    row = pltpu.roll(row, L - off, 1)
                if off + M > L:
                    after = d_ref[part, x, :, (tile + 1) * L : (tile + 2) * L]
                    row = jnp.where(lane < L - off, row, pltpu.roll(after, L - off, 1))
                mat[part, pl.ds(base + i, LOCAL_Y, stride=M), :] = row
        rows = [pl.ds(pl.multiple_of(base + k * M, M), M) for k in range(LOCAL_Y)]
        results = invert([(mat[0, r, :], mat[1, r, :]) for r in rows])
        for r, result in zip(rows, results):
            mat[0, r, :] = result[:, :L]
            mat[1, r, :] = result[:, L:]
        return carry

    sources = (s0, s1, s2, t0, t1)
    places = (r0, r1, r2, v0, v1)

    def exchange(c):
        src, dst = sources[c], places[c]
        used = pl.ds(0, USED[c])
        own = pltpu.make_async_copy(src.at[me, used], dst.at[me, used], rsem.at[c])
        own.start()

        def send(o, carry):
            z, x, y, h = qx >> 2, (qx & 3) + (o & 3), (qy >> 1) + (o >> 2), qy & 1
            for n in range(8):
                k, core = n & 3, n >> 2
                tx = (((z + k) & 3) << 2) | ((x + k) & 3)
                ty = (((y + k) & 3) << 1) | (h ^ core)
                target = (tx << 3) | ty

                def start():
                    pltpu.make_async_remote_copy(
                        src_ref=src.at[target, used],
                        dst_ref=dst.at[me, used],
                        send_sem=ssem.at[c],
                        recv_sem=rsem.at[c],
                        device_id=(tx, ty),
                        device_id_type=MESH,
                    ).start()

                if n == 0:
                    pl.when(target != me)(start)
                else:
                    start()
            return carry

        lax.fori_loop(0, NDEV // 8, send, 0)

    def arrived(c):
        whole = places[c].at[pl.ds(0, NDEV), pl.ds(0, USED[c])]
        pltpu.make_async_copy(whole, whole, rsem.at[c]).wait()

    def sent(c):
        whole = sources[c].at[pl.ds(0, NDEV - 1), pl.ds(0, USED[c])]
        pltpu.make_async_copy(whole, whole, ssem.at[c]).wait()

    def flat(ref, c):
        return ref.reshape((NDEV + 1) * PITCH[c], L)

    def pack(half, u):
        for v in range(4):
            for part in range(2):
                first = half * HALF * M + 4 * GROUPS * u + v
                block = jnp.concatenate(
                    [mat[part, pl.ds(first + 4 * g, HALF, stride=M), :] for g in range(GROUPS)], axis=0
                ).T
                for w in range(3):
                    lo, hi = max(0, w * L - v * M), min(M, (w + 1) * L - v * M)
                    if lo >= hi:
                        continue
                    row = 3 * u + w
                    if half == 0:
                        c, row = 0, part * 9 + row
                    elif row < 4:
                        c, row = 1, part * 4 + row
                    else:
                        c, row = 2, part * 5 + row - 4
                    at = (v * M + lo - w * L) * PITCH[c] + row
                    flat(sources[c], c)[pl.ds(at, hi - lo, stride=PITCH[c]), :] = block[lo:hi]

    def stage_one(row):
        c, first, count = (1, row, 4) if row < 4 else (2, row - 4, 5)
        cols = []
        for src, at, step in ((0, row, 9), (c, first, count)):
            ref = flat(places[src], src)
            cols.append(
                jnp.concatenate(
                    [ref[pl.ds(part * step + at, NDEV, stride=PITCH[src]), :] for part in range(2)], axis=0
                )
            )
        high, low = split(jnp.concatenate(cols, axis=1))
        table = first_ref[...]
        both = dot(table, high)
        total = both[: 2 * L] + both[2 * L :] + dot(table[: 2 * L], low)
        turned = []
        for bh in range(2):
            real, imag = total[:L, bh * L : (bh + 1) * L], total[L:, bh * L : (bh + 1) * L]
            tr, ti = twiddle_ref[bh, 0], twiddle_ref[bh, 1]
            turned.append(jnp.concatenate([real * tr - imag * ti, real * ti + imag * tr], axis=1))
        return turned[0] + turned[1], turned[0] - turned[1]

    def keep(row, at, pitch):
        for j0, value in enumerate(stage_one(row)):
            high, low = split(value)
            for c0 in range(4):
                rows = slice(c0 * pitch + at, c0 * pitch + at + Q)
                up_h[j0, rows, :] = high[c0 * Q : (c0 + 1) * Q]
                up_l[j0, rows, :] = low[c0 * Q : (c0 + 1) * Q]

    def stage_two(j0, rows):
        table = second_ref[j0]
        both = dot(table, up_h[j0, rows, :], 1)
        return both[: 2 * L] + both[2 * L :] + dot(table[: 2 * L], up_l[j0, rows, :], 1)

    def put(c, jx, c0, row, value):
        at = (4 * jx + c0) * LOCAL_Y * PITCH[c] + row
        flat(sources[c], c)[pl.ds(at, LOCAL_Y, stride=PITCH[c]), :] = value

    def transform(n):
        c = 3 + n
        for k in range(4):
            keep(4 * n + k, k * Q, L)
        for j0 in range(2):
            for pair in range(2):
                result = stage_two(j0, slice(pair * 2 * L, (pair + 1) * 2 * L))
                for part in range(2):
                    for g in range(GROUPS):
                        for j1 in range(2):
                            r = part * L + g * HALF + j1 * LOCAL_Y
                            for k in range(2):
                                put(
                                    c, 2 * j1 + j0, 2 * pair + k, part * GROUPS + g,
                                    result[r : r + LOCAL_Y, k * L : (k + 1) * L],
                                )
        if n == 0:
            return
        keep(8, 0, Q)
        lane = lax.broadcasted_iota(jnp.int32, (LOCAL_Y, L), 1)
        for j0 in range(2):
            result = stage_two(j0, slice(0, L))
            for part in range(2):
                for gh in range(2):
                    for j1 in range(2):
                        r = part * L + gh * 4 * HALF + j1 * LOCAL_Y
                        parts = [result[r + gl * HALF : r + gl * HALF + LOCAL_Y] for gl in range(4)]
                        for c0 in range(4):
                            row = parts[c0]
                            for gl in range(4):
                                if gl != c0:
                                    moved = pltpu.roll(parts[gl], (gl - c0) % 4 * Q, 1)
                                    row = jnp.where(lane // Q == gl, moved, row)
                            put(c, 2 * j1 + j0, c0, 2 * GROUPS + part * 2 + gh, row)

    def place(part, g, row, block):
        tile = 24 * (row // 3) + 3 * g + row % 3
        out_ref[part, :, :, tile * L : (tile + 1) * L] = block.reshape(LOCAL_X, LOCAL_Y, L)

    def finish(n):
        c = 3 + n
        src = flat(places[c], c)
        for part in range(2):
            for g in range(GROUPS):
                block = src[pl.ds(part * GROUPS + g, NDEV, stride=PITCH[c]), :].T
                for k in range(4):
                    place(part, g, 4 * n + k, block[k * Q : (k + 1) * Q])
            if n == 1:
                for gh in range(2):
                    block = src[pl.ds(2 * GROUPS + part * 2 + gh, NDEV, stride=PITCH[c]), :].T
                    for gl in range(4):
                        place(part, 4 * gh + gl, 8, block[gl * Q : (gl + 1) * Q])

    lax.fori_loop(0, LOCAL_X // 2, invert_some, 0)
    for u in range(3):
        pack(0, u)
    all_entered()
    exchange(0)
    lax.fori_loop(LOCAL_X // 2, LOCAL_X, invert_some, 0)
    pack(1, 0)
    pack(1, 1)
    exchange(1)
    pack(1, 2)
    exchange(2)
    for copy in constants:
        copy.wait()
    arrived(0)
    for n in range(2):
        arrived(1 + n)
        transform(n)
        exchange(3 + n)
    for n in range(2):
        arrived(3 + n)
        finish(n)
    for c in range(5):
        sent(c)


def per_device(dynamical):
    constants = tables()
    operands = [
        pltpu.with_memory_space_constraint(operand, pltpu.HBM)
        for operand in (dynamical, *map(jnp.asarray, constants))
    ]
    buffers = [pltpu.VMEM((NDEV + 1, p, L), F32) for p in PITCH]
    return pl.pallas_call(
        kernel,
        out_shape=pltpu.VMEM(dynamical.shape, F32),
        in_specs=[pl.BlockSpec(memory_space=pltpu.HBM)] * 4,
        out_specs=pl.BlockSpec(memory_space=pltpu.VMEM),
        scratch_shapes=[
            pltpu.VMEM(dynamical.shape, F32),
            *[pltpu.VMEM(table.shape, table.dtype) for table in constants],
            pltpu.VMEM((2, (Q + 1) * M, L), F32),
            *buffers, *buffers,
            pltpu.VMEM((2, 4 * L, 2 * L), BF16),
            pltpu.VMEM((2, 4 * L, 2 * L), BF16),
            pltpu.SemaphoreType.DMA((5,)),
            pltpu.SemaphoreType.DMA((5,)),
            pltpu.SemaphoreType.DMA((LOCAL_X,)),
            pltpu.SemaphoreType.DMA((3,)),
            pltpu.SemaphoreType.REGULAR,
        ],
        compiler_params=pltpu.CompilerParams(
            collective_id=0, has_side_effects=True, vmem_limit_bytes=48 << 20
        ),
    )(*operands)


def solution(mesh):
    return jax.shard_map(
        per_device,
        mesh=mesh,
        in_specs=(P(None, "qx", "qy", None),),
        out_specs=P(None, "qx", "qy", None),
        check_vma=False,
    )
```

```python
import functools

import jax
import jax.numpy as jnp
import ml_dtypes
import numpy as np
from jax import lax
from jax.experimental import pallas as pl
from jax.experimental.pallas import tpu as pltpu
from jax.sharding import PartitionSpec as P

M = 96
ETA = 0.25
NDEV = 128
SIZE_X, SIZE_Y = 16, 8
LOCAL_X, LOCAL_Y = 4, 8
Q = LOCAL_X * LOCAL_Y
L = 128
HALF = Q // 2
GROUPS = L // HALF
USED = (18, 8, 10, 16, 20)
PITCH = (24, 8, 16, 16, 24)
MESH = pl.DeviceIdType.MESH
F32 = jnp.float32
BF16 = jnp.bfloat16


def split_table(table):
    high = table.astype(ml_dtypes.bfloat16)
    low = (table - high.astype(np.float64)).astype(ml_dtypes.bfloat16)
    return high, low


def embed_table(angle):
    cosine, sine = np.cos(angle), np.sin(angle)
    return np.block([[cosine, -sine], [sine, cosine]])


def tables():
    ax, ay = np.divmod(np.arange(NDEV), SIZE_Y)
    turns = (ax[:, None] * ax[None, :] % 16) / 16 + (ay[:, None] * ay[None, :] % 8) / 8
    first = np.concatenate(split_table(embed_table(2 * np.pi * turns)), axis=0)
    lane = np.arange(L)
    group, bl, by = lane // HALF, lane % HALF // LOCAL_Y, lane % LOCAL_Y
    turns = np.stack(
        [
            (ax[:, None] * (2 * bh + bl)[None, :] + ay[:, None] * by[None, :]) / 64
            for bh in range(2)
        ]
    )
    twiddle = np.stack([np.cos(2 * np.pi * turns), np.sin(2 * np.pi * turns)], axis=1) / 64
    same = group[:, None] == group[None, :]
    second = []
    for j0 in range(2):
        turns = (2 * bl + j0)[:, None] * bl[None, :] / 4 + (by[:, None] * by[None, :] % 8) / 8
        cosine, sine = np.cos(2 * np.pi * turns) * same, np.sin(2 * np.pi * turns) * same
        table = split_table(np.block([[cosine, -sine], [sine, cosine]]))
        second.append(np.concatenate(table, axis=0))
    return first, twiddle.astype(np.float32), np.stack(second)


def split(value):
    high = value.astype(BF16)
    low = (value - high.astype(F32)).astype(BF16)
    return high, low


def dot(a, b, contract=0):
    return lax.dot_general(a, b, (((1,), (contract,)), ((), ())), preferred_element_type=F32)


def embed(part):
    zeros = jnp.zeros((L - M, 2 * L), part.dtype)
    real, imag = part[:, :L], part[:, L:]
    return jnp.concatenate(
        [part, zeros, jnp.concatenate([-imag, real], axis=1), zeros], axis=0
    )


def product(left, right):
    n = left[0].shape[0]
    both = dot(jnp.concatenate(left, axis=0), embed(right[0]))
    return both[:n] + both[n:] + dot(left[0], embed(right[1]))


def begin(real, imag):
    row = lax.broadcasted_iota(jnp.int32, (M, L), 0)
    col = lax.broadcasted_iota(jnp.int32, (M, L), 1)
    eye = row == col
    off = (col < M) & (row != col)
    diag = jnp.where(eye, real, 0.0)

    def start(d):
        denom = d * d + ETA * ETA
        return d / denom, -ETA / denom

    cr, ci = start(jnp.sum(diag, axis=0, keepdims=True))
    rr, ri = start(jnp.sum(diag, axis=1, keepdims=True))
    er = jnp.where(off, imag * ci - real * cr, 0.0)
    ei = jnp.where(off, -(real * ci + imag * cr), 0.0)
    pr = jnp.where(eye, 1.0, er)
    x1 = jnp.concatenate([rr * pr - ri * ei, rr * ei + ri * pr], axis=1)
    return x1, split(jnp.concatenate([er, ei], axis=1))


def stack(a, b):
    return tuple(jnp.concatenate(pair, axis=0) for pair in zip(a, b))


def invert(matrices):
    x1, e0 = zip(*[begin(*m) for m in matrices])
    e1 = [split(product(e, e)) for e in e0]
    both = [product(stack(split(x), e), e) for x, e in zip(x1, e1)]
    x2 = [x + b[:M] for x, b in zip(x1, both)]
    return [x + product(split(x), split(b[M:])) for x, b in zip(x2, both)]


def kernel(
    d_hbm, first_hbm, twiddle_hbm, second_hbm, out_ref,
    d_ref, first_ref, twiddle_ref, second_ref,
    mat, s0, s1, s2, t0, t1, r0, r1, r2, v0, v1, up_h, up_l, ssem, rsem, dsem, csem, both_sem,
):
    qx = lax.axis_index("qx")
    qy = lax.axis_index("qy")
    me = qx * SIZE_Y + qy

    def fetch(x):
        return pltpu.make_async_copy(d_hbm.at[:, x], d_ref.at[:, x], dsem.at[x])

    for x in range(LOCAL_X):
        fetch(x).start()
    constants = [
        pltpu.make_async_copy(first_hbm, first_ref, csem.at[0]),
        pltpu.make_async_copy(twiddle_hbm, twiddle_ref, csem.at[1]),
        pltpu.make_async_copy(second_hbm, second_ref, csem.at[2]),
    ]
    for copy in constants:
        copy.start()

    barrier = pltpu.get_barrier_semaphore()

    def hops(o):
        return sum((0, 1, 2, 1)[o >> n & 3] for n in (1, 3, 5))

    for o in [*sorted(range(2, NDEV, 2), key=hops, reverse=True), 1]:
        other = jnp.bitwise_xor(me, o)
        pl.semaphore_signal(
            barrier, inc=1, device_id=(other >> 3, other & 7), device_id_type=MESH
        )

    def all_entered():
        pl.semaphore_wait(barrier, NDEV // 2)
        pl.semaphore_signal(
            both_sem, inc=1, device_id=(qx, jnp.bitwise_xor(qy, 1)), device_id_type=MESH
        )
        pl.semaphore_wait(both_sem, 1)

    def unflatten(x):
        fetch(x).wait()
        lane = lax.broadcasted_iota(jnp.int32, (LOCAL_Y, L), 1)
        base = x * (LOCAL_Y * M)
        for part in range(2):
            for i in range(M):
                tile, off = divmod(i * M, L)
                row = d_ref[part, x, :, tile * L : (tile + 1) * L]
                if off:
                    row = pltpu.roll(row, L - off, 1)
                if off + M > L:
                    after = d_ref[part, x, :, (tile + 1) * L : (tile + 2) * L]
                    row = jnp.where(lane < L - off, row, pltpu.roll(after, L - off, 1))
                mat[part, pl.ds(base + i, LOCAL_Y, stride=M), :] = row

    def invert_at(x):
        base = x * (LOCAL_Y * M)
        rows = [pl.ds(pl.multiple_of(base + k * M, M), M) for k in range(LOCAL_Y)]
        results = invert([(mat[0, r, :], mat[1, r, :]) for r in rows])
        for r, result in zip(rows, results):
            mat[0, r, :] = result[:, :L]
            mat[1, r, :] = result[:, L:]

    sources = (s0, s1, s2, t0, t1)
    places = (r0, r1, r2, v0, v1)

    def exchange(c):
        src, dst = sources[c], places[c]
        used = pl.ds(0, USED[c])
        own = pltpu.make_async_copy(src.at[me, used], dst.at[me, used], rsem.at[c])
        own.start()

        def send(o, carry):
            z, x, y, h = qx >> 2, (qx & 3) + (o & 3), (qy >> 1) + (o >> 2), qy & 1
            for n in range(8):
                k, core = n & 3, n >> 2
                tx = (((z + k) & 3) << 2) | ((x + k) & 3)
                ty = (((y + k) & 3) << 1) | (h ^ core)
                target = (tx << 3) | ty

                def start():
                    pltpu.make_async_remote_copy(
                        src_ref=src.at[target, used],
                        dst_ref=dst.at[me, used],
                        send_sem=ssem.at[c],
                        recv_sem=rsem.at[c],
                        device_id=(tx, ty),
                        device_id_type=MESH,
                    ).start()

                if n == 0:
                    pl.when(target != me)(start)
                else:
                    start()
            return carry

        lax.fori_loop(0, NDEV // 8, send, 0)

    def arrived(c):
        whole = places[c].at[pl.ds(0, NDEV), pl.ds(0, USED[c])]
        pltpu.make_async_copy(whole, whole, rsem.at[c]).wait()

    def sent(c):
        whole = sources[c].at[pl.ds(0, NDEV - 1), pl.ds(0, USED[c])]
        pltpu.make_async_copy(whole, whole, ssem.at[c]).wait()

    def flat(ref, c):
        return ref.reshape((NDEV + 1) * PITCH[c], L)

    def pack(half, u):
        for v in range(4):
            for part in range(2):
                first = half * HALF * M + 4 * GROUPS * u + v
                block = jnp.concatenate(
                    [mat[part, pl.ds(first + 4 * g, HALF, stride=M), :] for g in range(GROUPS)], axis=0
                ).T
                for w in range(3):
                    lo, hi = max(0, w * L - v * M), min(M, (w + 1) * L - v * M)
                    if lo >= hi:
                        continue
                    row = 3 * u + w
                    if half == 0:
                        c, row = 0, part * 9 + row
                    elif row < 4:
                        c, row = 1, part * 4 + row
                    else:
                        c, row = 2, part * 5 + row - 4
                    at = (v * M + lo - w * L) * PITCH[c] + row
                    flat(sources[c], c)[pl.ds(at, hi - lo, stride=PITCH[c]), :] = block[lo:hi]

    def stage_one(row):
        c, first, count = (1, row, 4) if row < 4 else (2, row - 4, 5)
        cols = []
        for src, at, step in ((0, row, 9), (c, first, count)):
            ref = flat(places[src], src)
            cols.append(
                jnp.concatenate(
                    [ref[pl.ds(part * step + at, NDEV, stride=PITCH[src]), :] for part in range(2)], axis=0
                )
            )
        high, low = split(jnp.concatenate(cols, axis=1))
        table = first_ref[...]
        both = dot(table, high)
        total = both[: 2 * L] + both[2 * L :] + dot(table[: 2 * L], low)
        turned = []
        for bh in range(2):
            real, imag = total[:L, bh * L : (bh + 1) * L], total[L:, bh * L : (bh + 1) * L]
            tr, ti = twiddle_ref[bh, 0], twiddle_ref[bh, 1]
            turned.append(jnp.concatenate([real * tr - imag * ti, real * ti + imag * tr], axis=1))
        return turned[0] + turned[1], turned[0] - turned[1]

    def keep(row, at, pitch):
        for j0, value in enumerate(stage_one(row)):
            high, low = split(value)
            for c0 in range(4):
                rows = slice(c0 * pitch + at, c0 * pitch + at + Q)
                up_h[j0, rows, :] = high[c0 * Q : (c0 + 1) * Q]
                up_l[j0, rows, :] = low[c0 * Q : (c0 + 1) * Q]

    def stage_two(j0, rows):
        table = second_ref[j0]
        both = dot(table, up_h[j0, rows, :], 1)
        return both[: 2 * L] + both[2 * L :] + dot(table[: 2 * L], up_l[j0, rows, :], 1)

    def put(c, jx, c0, row, value):
        at = (4 * jx + c0) * LOCAL_Y * PITCH[c] + row
        flat(sources[c], c)[pl.ds(at, LOCAL_Y, stride=PITCH[c]), :] = value

    def transform(n):
        c = 3 + n
        for k in range(4):
            keep(4 * n + k, k * Q, L)
        for j0 in range(2):
            for pair in range(2):
                result = stage_two(j0, slice(pair * 2 * L, (pair + 1) * 2 * L))
                for part in range(2):
                    for g in range(GROUPS):
                        for j1 in range(2):
                            r = part * L + g * HALF + j1 * LOCAL_Y
                            for k in range(2):
                                put(
                                    c, 2 * j1 + j0, 2 * pair + k, part * GROUPS + g,
                                    result[r : r + LOCAL_Y, k * L : (k + 1) * L],
                                )
        if n == 0:
            return
        keep(8, 0, Q)
        lane = lax.broadcasted_iota(jnp.int32, (LOCAL_Y, L), 1)
        for j0 in range(2):
            result = stage_two(j0, slice(0, L))
            for part in range(2):
                for gh in range(2):
                    for j1 in range(2):
                        r = part * L + gh * 4 * HALF + j1 * LOCAL_Y
                        parts = [result[r + gl * HALF : r + gl * HALF + LOCAL_Y] for gl in range(4)]
                        for c0 in range(4):
                            row = parts[c0]
                            for gl in range(4):
                                if gl != c0:
                                    moved = pltpu.roll(parts[gl], (gl - c0) % 4 * Q, 1)
                                    row = jnp.where(lane // Q == gl, moved, row)
                            put(c, 2 * j1 + j0, c0, 2 * GROUPS + part * 2 + gh, row)

    def place(part, g, row, block):
        tile = 24 * (row // 3) + 3 * g + row % 3
        out_ref[part, :, :, tile * L : (tile + 1) * L] = block.reshape(LOCAL_X, LOCAL_Y, L)

    def finish(n):
        c = 3 + n
        src = flat(places[c], c)
        for part in range(2):
            for g in range(GROUPS):
                block = src[pl.ds(part * GROUPS + g, NDEV, stride=PITCH[c]), :].T
                for k in range(4):
                    place(part, g, 4 * n + k, block[k * Q : (k + 1) * Q])
            if n == 1:
                for gh in range(2):
                    block = src[pl.ds(2 * GROUPS + part * 2 + gh, NDEV, stride=PITCH[c]), :].T
                    for gl in range(4):
                        place(part, 4 * gh + gl, 8, block[gl * Q : (gl + 1) * Q])

    unflatten(0)
    unflatten(1)
    invert_at(0)
    invert_at(1)
    for u in range(3):
        pack(0, u)
    all_entered()
    exchange(0)
    def rest(x, carry):
        unflatten(x)
        invert_at(x)
        return carry

    lax.fori_loop(LOCAL_X // 2, LOCAL_X, rest, 0)
    pack(1, 0)
    pack(1, 1)
    exchange(1)
    pack(1, 2)
    exchange(2)
    for copy in constants:
        copy.wait()
    arrived(0)
    for n in range(2):
        arrived(1 + n)
        transform(n)
        exchange(3 + n)
    for n in range(2):
        arrived(3 + n)
        finish(n)
    for c in range(5):
        sent(c)


def per_device(dynamical):
    constants = tables()
    operands = [
        pltpu.with_memory_space_constraint(operand, pltpu.HBM)
        for operand in (dynamical, *map(jnp.asarray, constants))
    ]
    buffers = [pltpu.VMEM((NDEV + 1, p, L), F32) for p in PITCH]
    return pl.pallas_call(
        kernel,
        out_shape=pltpu.VMEM(dynamical.shape, F32),
        in_specs=[pl.BlockSpec(memory_space=pltpu.HBM)] * 4,
        out_specs=pl.BlockSpec(memory_space=pltpu.VMEM),
        scratch_shapes=[
            pltpu.VMEM(dynamical.shape, F32),
            *[pltpu.VMEM(table.shape, table.dtype) for table in constants],
            pltpu.VMEM((2, (Q + 1) * M, L), F32),
            *buffers, *buffers,
            pltpu.VMEM((2, 4 * L, 2 * L), BF16),
            pltpu.VMEM((2, 4 * L, 2 * L), BF16),
            pltpu.SemaphoreType.DMA((5,)),
            pltpu.SemaphoreType.DMA((5,)),
            pltpu.SemaphoreType.DMA((LOCAL_X,)),
            pltpu.SemaphoreType.DMA((3,)),
            pltpu.SemaphoreType.REGULAR,
        ],
        compiler_params=pltpu.CompilerParams(
            collective_id=0, has_side_effects=True, vmem_limit_bytes=48 << 20
        ),
    )(*operands)


def solution(mesh):
    return jax.shard_map(
        per_device,
        mesh=mesh,
        in_specs=(P(None, "qx", "qy", None),),
        out_specs=P(None, "qx", "qy", None),
        check_vma=False,
    )
```
